512 devices in a mesh: kv: 8 (over z_lo), pb: 8 (over x, z_hi), rep: 8 (over y, core).
Axes of the slice: x: 4, y: 4, z: 16 (z_hi: 2, z_lo: 8; z = z_hi * 8 + z_lo), core: 2. Of those that a mesh axis runs over, the one named last changes fastest.
Arguments:
- queries: bfloat16 [320, 64, 128], P('rep', ('kv', 'pb')), may hold values from -8 to 8
- prefix_cache: bfloat16 [8, 2, 4096, 128], P('kv', None, ('pb', 'rep')), may hold values from -8 to 8
- suffix_cache: bfloat16 [320, 8, 2, 512, 128], P('rep', 'kv', None, 'pb'), may hold values from -8 to 8
- suffix_lengths: int32 [320], P('rep'), may hold values from 1 to 512, as said below
- residual: float32 [320, 8192], P(('kv', 'pb'), 'rep'), may hold values from -120 to 120
- norm_gain: float32 [8192], P('rep'), may hold values from 0.1 to 1.9
- out_weight: bfloat16 [8192, 8192], P(('kv', 'pb'), 'rep'), may hold values from -0.5 to 0.5
- gate_weight: bfloat16 [8192, 29568], P('rep', ('kv', 'pb')), may hold values from -0.0625 to 0.0625
- up_weight: bfloat16 [8192, 29568], P('rep', ('kv', 'pb')), may hold values from -0.0625 to 0.0625
- down_weight: bfloat16 [29568, 8192], P(('kv', 'pb'), 'rep'), may hold values from -0.375 to 0.375
Outputs:
- context: bfloat16 [320, 64, 128], P('rep', ('kv', 'pb'))
- layer_out: float32 [320, 8192], P(('kv', 'pb'), 'rep')
The draws below stay inside these ranges and needn't reach their ends.
Inputs may be any that keep to these rules, and one draw needn't show every extreme that they name: `suffix_lengths`: some row has exactly 512 live suffix positions.
All inputs are finite; a program needn't handle non-finite values.
Results may differ from the reference program's by a relative error of at most 0.024.
Values may be sent and summed in bfloat16 or wider, within the bound.
No kernel may reach another device: no remote copies, remote signals or barrier semaphores. Data moves between devices by JAX's collectives and lax.ppermute only.
A program may use at most 64 MiB of HBM per device.

```python
import math
import jax
import jax.numpy as jnp
from jax import lax

D = 8192
FF = 29568
HEAD_DIM = 128
KV_HEADS = 8
GROUP = 8
HEADS = 64
SUFFIX = 512
PREFIX = 4096
ROWS = 320


def draw_queries(key, part):
    key = jax.random.fold_in(key, 1)
    array_shape = (ROWS, HEADS, HEAD_DIM)
    query_field = 2.5 * jax.random.truncated_normal(key, -3.2, 3.2, array_shape, jnp.float32)
    return query_field.astype(jnp.bfloat16)


def draw_prefix_cache(key, part):
    key = jax.random.fold_in(key, 2)
    array_shape = (KV_HEADS, PREFIX, HEAD_DIM)
    key_rows = jax.random.truncated_normal(jax.random.fold_in(key, 1), -6.0, 6.0, array_shape, jnp.float32)
    value_rows = 2.0 * jax.random.truncated_normal(jax.random.fold_in(key, 2), -4.0, 4.0, array_shape, jnp.float32)
    return jnp.stack([key_rows, value_rows], axis=1).astype(jnp.bfloat16)


def draw_suffix_lengths(key, part):
    key = jax.random.fold_in(key, 3)
    drawn_lengths = jax.random.randint(jax.random.fold_in(key, 1), (ROWS,), 1, SUFFIX + 1)
    longest = jax.random.randint(jax.random.fold_in(key, 2), (), 0, ROWS)
    return jnp.where(jnp.arange(ROWS) == longest, SUFFIX, drawn_lengths).astype(jnp.int32)


def draw_residual(key, part):
    key = jax.random.fold_in(key, 4)
    column_rise = 3.0 ** (jnp.arange(D, dtype=jnp.float32) / D - 0.5)
    low_end = 0.4
    noise_field = jax.random.truncated_normal(jax.random.fold_in(key, 1), -4.0, 4.0, (ROWS, D), jnp.float32)
    high_end = 4.0
    row_scale = jnp.exp(jax.random.uniform(jax.random.fold_in(key, 2), (ROWS, 1), jnp.float32, math.log(low_end), math.log(high_end)))
    column_scale = jnp.exp(jax.random.uniform(jax.random.fold_in(key, 3), (1, D), jnp.float32, math.log(low_end), math.log(high_end))) * column_rise[None, :]
    return (noise_field * row_scale * column_scale).astype(jnp.float32)


def levels(own_key, dims, shards, smallest, high):
    gain = 1.0
    for dim, shards_of in shards:
        steps = jax.random.uniform(jax.random.fold_in(jax.random.fold_in(own_key, 6), dim), (shards_of,), jnp.float32, smallest / len(shards), high / len(shards))
        gain = gain * jnp.repeat(jnp.exp(steps), dims[dim] // shards_of).reshape((-1,) + (1,) * (len(dims) - 1 - dim))
    return gain


def noise(stream_key, dims, spread, limit, split=(), held_as=jnp.bfloat16):
    gain = levels(stream_key, dims, split, -0.22, 0.18) if split else 1.0
    array = jax.random.normal(stream_key, dims, jnp.float32) * spread * gain
    return jnp.minimum(jnp.maximum(array, -limit), limit).astype(held_as)


def setup_inputs(seed: int = 0) -> dict:
    keys = jax.random.split(jax.random.key(seed), 11)
    queries = draw_queries(jax.random.fold_in(keys[10], 71), 0)
    prefix_cache = draw_prefix_cache(jax.random.fold_in(keys[10], 71), 0)
    suffix_cache = noise(keys[2], (ROWS, KV_HEADS, 2, SUFFIX, HEAD_DIM), 1.5, 8.0, ((0, 8), (1, 8), (3, 8)))
    suffix_lengths = draw_suffix_lengths(jax.random.fold_in(keys[10], 71), 0)
    residual = draw_residual(jax.random.fold_in(keys[10], 71), 0)
    norm_gain = jnp.clip(1.0 + 0.18 * jax.random.normal(keys[5], (D,), jnp.float32), 0.1, 1.9)
    out_weight = noise(keys[6], (HEADS * HEAD_DIM, D), HEAD_DIM ** -0.5, 0.5, ((0, 64), (1, 8)))
    gate_weight = noise(keys[7], (D, FF), D ** -0.5, 0.0625, ((0, 8), (1, 64)))
    up_weight = noise(keys[8], (D, FF), D ** -0.5, 0.0625, ((0, 8), (1, 64)))
    down_weight = noise(keys[9], (FF, D), (FF // (2 * KV_HEADS * GROUP)) ** -0.5, 0.375, ((0, 64), (1, 8)))
    return {"queries": queries, "prefix_cache": prefix_cache, "suffix_cache": suffix_cache, "suffix_lengths": suffix_lengths, "residual": residual, "norm_gain": norm_gain, "out_weight": out_weight, "gate_weight": gate_weight, "up_weight": up_weight, "down_weight": down_weight}


lowest = -1e+30
epsilon = 1e-06

def group_attention(group_args):
    group_queries, prefix_keys, prefix_values, suffix_keys, suffix_values, all_lengths = group_args
    score_scale = HEAD_DIM ** (-0.5)
    query_float = group_queries.astype(jnp.float32)
    prefix_scores = jnp.einsum('rgd,td->rgt', query_float, prefix_keys.astype(jnp.float32)) * score_scale
    suffix_scores = jnp.einsum('rgd,rsd->rgs', query_float, suffix_keys.astype(jnp.float32)) * score_scale
    is_live = (lax.broadcasted_iota(jnp.int32, (ROWS, SUFFIX), 1) < all_lengths[:, None])[:, None, :]
    suffix_scores = jnp.where(is_live, suffix_scores, lowest)
    highest = jnp.maximum(lax.optimization_barrier(jnp.max(prefix_scores, axis=2)), lax.optimization_barrier(jnp.max(suffix_scores, axis=2)))
    prefix_weights = jnp.exp(prefix_scores - highest[..., None])
    suffix_weights = jnp.where(is_live, jnp.exp(suffix_scores - highest[..., None]), 0.0)
    denoms = lax.optimization_barrier(jnp.sum(prefix_weights, axis=2)) + lax.optimization_barrier(jnp.sum(suffix_weights, axis=2))
    prefix_round = lax.optimization_barrier(prefix_weights.astype(jnp.bfloat16))
    suffix_round = lax.optimization_barrier(suffix_weights.astype(jnp.bfloat16))
    numers = jnp.einsum('rgt,td->rgd', prefix_round.astype(jnp.float32), prefix_values.astype(jnp.float32))
    numers = numers + jnp.einsum('rgs,rsd->rgd', suffix_round.astype(jnp.float32), suffix_values.astype(jnp.float32))
    return (numers / denoms[..., None]).astype(jnp.bfloat16)

def reference(queries, prefix_cache, suffix_cache, suffix_lengths, residual, norm_gain, out_weight, gate_weight, up_weight, down_weight):
    grouped = queries.reshape(ROWS, KV_HEADS, GROUP, HEAD_DIM).transpose(1, 0, 2, 3)
    suffix_keys = suffix_cache[:, :, 0].transpose(1, 0, 2, 3)
    suffix_values = suffix_cache[:, :, 1].transpose(1, 0, 2, 3)
    all_lengths = jnp.broadcast_to(suffix_lengths, (KV_HEADS, ROWS))
    context = lax.map(group_attention, (grouped, prefix_cache[:, 0], prefix_cache[:, 1], suffix_keys, suffix_values, all_lengths))
    context = context.transpose(1, 0, 2, 3).reshape(ROWS, HEADS, HEAD_DIM)
    attended = jnp.dot(context.reshape(ROWS, HEADS * HEAD_DIM), out_weight, preferred_element_type=jnp.float32)
    mixed = residual + attended
    normed = (mixed * lax.rsqrt(lax.optimization_barrier(jnp.mean(mixed * mixed, axis=1, keepdims=True)) + epsilon) * norm_gain).astype(jnp.bfloat16)
    gate_sums = jnp.dot(normed, gate_weight, preferred_element_type=jnp.float32)
    up_sums = jnp.dot(normed, up_weight, preferred_element_type=jnp.float32)
    hidden = (jax.nn.silu(gate_sums) * up_sums).astype(jnp.bfloat16)
    layer_out = mixed + jnp.dot(hidden, down_weight, preferred_element_type=jnp.float32)
    return (context, layer_out)
```

```python
import jax
import jax.numpy as jnp
from jax import lax
from jax.sharding import PartitionSpec as P

D = 8192
HEAD_DIM = 128
X = 4
ZH = 2

lowest = -1e30
epsilon = 1e-06
f32 = jnp.float32
bf16 = jnp.bfloat16

x_groups = [[x * ZH + zh for x in range(X)] for zh in range(ZH)]
z_groups = [[kv * 8 + x * ZH + zh for kv in range(8) for zh in range(ZH)] for x in range(X)]


def exchange(blocks, axes, groups=None):
    return lax.all_to_all(blocks, axes, 0, 0, axis_index_groups=groups, tiled=True)


def spread(block, count, axes, groups=None):
    return exchange(jnp.broadcast_to(block[None], (count,) + block.shape), axes, groups)


def split_float(value):
    high = lax.reduce_precision(value, 8, 7)
    rest = value - high
    middle = lax.reduce_precision(rest, 8, 7)
    return high.astype(bf16), middle.astype(bf16), (rest - middle).astype(bf16)


def local_attention(queries, prefix, suffix, lengths, offset):
    scale = HEAD_DIM ** (-0.5)
    heads, rows, width = queries.shape
    shared = jnp.einsum("grd,td->grt", queries, prefix[0], preferred_element_type=f32) * scale
    own = jnp.einsum("grd,rsd->grs", queries, suffix[:, 0], preferred_element_type=f32) * scale
    position = offset + lax.broadcasted_iota(jnp.int32, (rows, suffix.shape[2]), 1)
    is_live = (position < lengths[:, None])[None]
    own = jnp.where(is_live, own, lowest)
    highest = jnp.maximum(jnp.max(shared, axis=2), jnp.max(own, axis=2))
    shared_weights = jnp.exp(shared - highest[..., None])
    own_weights = jnp.where(is_live, jnp.exp(own - highest[..., None]), 0.0)
    denoms = jnp.sum(shared_weights, axis=2) + jnp.sum(own_weights, axis=2)
    numers = jnp.einsum(
        "grt,td->grd", shared_weights.astype(bf16), prefix[1], preferred_element_type=f32
    ) + jnp.einsum(
        "grs,rsd->grd", own_weights.astype(bf16), suffix[:, 1], preferred_element_type=f32
    )
    return highest, denoms, numers


def sum_over_owners(partial):
    rows, n = partial.shape
    over_x = exchange(partial.astype(bf16).reshape(X, rows // X, n), "pb", x_groups)
    over_x = jnp.sum(over_x.astype(f32), axis=0)
    over_z = exchange(over_x.astype(bf16).reshape(16, rows // 64, n), ("kv", "pb"), z_groups)
    return jnp.sum(over_z.astype(f32), axis=0)


def per_device(
    queries,
    prefix_cache,
    suffix_cache,
    suffix_lengths,
    residual,
    norm_gain,
    out_weight,
    gate_weight,
    up_weight,
    down_weight,
):
    rows, _, width = queries.shape
    units = gate_weight.shape[1]
    prefix = lax.all_gather(prefix_cache[0], "rep", axis=1, tiled=True)
    group_queries = spread(queries[:, 0, :], 8, "pb")
    offset = lax.axis_index("pb") * suffix_cache.shape[3]
    highest, denoms, numers = local_attention(
        group_queries, prefix, suffix_cache[:, 0], suffix_lengths, offset
    )
    logs = highest + jnp.log(denoms)
    stats = jnp.pad(jnp.stack(split_float(logs), axis=1), ((0, 0), (0, 5), (0, width - rows)))
    parts = jnp.concatenate([(numers / denoms[..., None]).astype(bf16), stats], axis=1)
    parts = exchange(parts, "pb").astype(f32)
    logs = jnp.sum(parts[:, rows : rows + 3, :rows], axis=1)
    factor = jnp.exp(logs - jnp.max(logs, axis=0))
    factor = factor / jnp.sum(factor, axis=0)
    context = jnp.sum(parts[:, :rows] * factor[..., None], axis=0).astype(bf16)

    all_context = spread(context, 8, "rep").reshape(8, X, rows // X, width)
    all_context = all_context.transpose(1, 0, 2, 3).reshape(8 * rows, width)
    attended = jnp.dot(all_context, out_weight, preferred_element_type=f32)
    mixed = residual + sum_over_owners(attended)

    squares = jnp.sum(mixed * mixed, axis=1, keepdims=True)
    squares = jnp.concatenate(split_float(squares), axis=1)
    sent = jnp.concatenate(
        [(mixed * norm_gain).astype(bf16), jnp.pad(squares, ((0, 0), (0, 125)))], axis=1
    )
    sent = spread(sent, 16, ("kv", "pb"), z_groups).reshape(2 * rows, -1)
    sent = spread(sent, X, "pb", x_groups).reshape(8 * rows, -1)
    scaled, squares = sent[:, : mixed.shape[1]], sent[:, mixed.shape[1] : mixed.shape[1] + 3]
    gates = jnp.dot(scaled, gate_weight, preferred_element_type=f32).astype(bf16)
    ups = jnp.dot(scaled, up_weight, preferred_element_type=f32).astype(bf16)
    partial = jnp.concatenate(
        [
            jnp.pad(jnp.concatenate([gates, squares], axis=1), ((0, 0), (0, 512 - units - 3))),
            jnp.pad(ups, ((0, 0), (0, 512 - units))),
        ],
        axis=1,
    )
    summed = jnp.sum(exchange(partial.reshape(8, rows, 1024), "rep").astype(f32), axis=0)
    inverse = lax.rsqrt(jnp.sum(summed[:, units : units + 3], axis=1, keepdims=True) / D + epsilon)
    gates = summed[:, :units] * inverse
    ups = summed[:, 512 : 512 + units] * inverse
    hidden = (jax.nn.silu(gates) * ups).astype(bf16)
    hidden = spread(hidden, 8, "rep").reshape(8 * rows, units)
    layer_out = mixed + sum_over_owners(jnp.dot(hidden, down_weight, preferred_element_type=f32))
    return (context[:, None, :], layer_out)


def solution(mesh):
    in_specs = (
        P("rep", ("kv", "pb"), None),
        P("kv", None, ("pb", "rep"), None),
        P("rep", "kv", None, "pb", None),
        P("rep"),
        P(("kv", "pb"), "rep"),
        P("rep"),
        P(("kv", "pb"), "rep"),
        P("rep", ("kv", "pb")),
        P("rep", ("kv", "pb")),
        P(("kv", "pb"), "rep"),
    )
    out_specs = (P("rep", ("kv", "pb"), None), P(("kv", "pb"), "rep"))
    return jax.shard_map(
        per_device, mesh=mesh, in_specs=in_specs, out_specs=out_specs, check_vma=False
    )
```

```python
import functools

import jax
import jax.numpy as jnp
from jax import lax
from jax.experimental import pallas as pl
from jax.experimental.pallas import tpu as pltpu
from jax.sharding import PartitionSpec as P

D = 8192
HEAD_DIM = 128
X = 4
ZH = 2
Z = 16
LANES = 128

lowest = -1e30
epsilon = 1e-06
f32 = jnp.float32
bf16 = jnp.bfloat16

x_groups = [[x * ZH + zh for x in range(X)] for zh in range(ZH)]
z_groups = [[kv * 8 + x * ZH + zh for zh in range(ZH) for kv in range(8)] for x in range(X)]


def exchange(blocks, axes, groups=None):
    return lax.all_to_all(blocks, axes, 0, 0, axis_index_groups=groups, tiled=True)


def spread(block, count, axes, groups=None):
    return exchange(jnp.broadcast_to(block[None], (count,) + block.shape), axes, groups)


def split_float(value):
    high = lax.reduce_precision(value, 8, 7)
    rest = value - high
    middle = lax.reduce_precision(rest, 8, 7)
    return high.astype(bf16), middle.astype(bf16), (rest - middle).astype(bf16)


def local_attention(queries, prefix, suffix, lengths, offset):
    scale = HEAD_DIM ** (-0.5)
    heads, rows, width = queries.shape
    shared = jnp.einsum("grd,td->grt", queries, prefix[0], preferred_element_type=f32) * scale
    own = jnp.einsum("grd,rsd->grs", queries, suffix[:, 0], preferred_element_type=f32) * scale
    position = offset + lax.broadcasted_iota(jnp.int32, (rows, suffix.shape[2]), 1)
    is_live = (position < lengths[:, None])[None]
    own = jnp.where(is_live, own, lowest)
    highest = jnp.maximum(jnp.max(shared, axis=2), jnp.max(own, axis=2))
    shared_weights = jnp.exp(shared - highest[..., None])
    own_weights = jnp.where(is_live, jnp.exp(own - highest[..., None]), 0.0)
    denoms = jnp.sum(shared_weights, axis=2) + jnp.sum(own_weights, axis=2)
    numers = jnp.einsum(
        "grt,td->grd", shared_weights.astype(bf16), prefix[1], preferred_element_type=f32
    ) + jnp.einsum(
        "grs,rsd->grd", own_weights.astype(bf16), suffix[:, 1], preferred_element_type=f32
    )
    return highest, denoms, numers


def gate_up_body(rows_ref, inverse_gain_ref, gate_ref, up_ref, out_ref):
    units = gate_ref.shape[0]
    contract = (((1,), (1,)), ((), ()))
    rows = rows_ref[...]
    gates = lax.dot_general(rows, gate_ref[...], contract, preferred_element_type=f32)
    out_ref[:, :units] = gates.astype(bf16)
    ups = lax.dot_general(rows, up_ref[...], contract, preferred_element_type=f32)
    out_ref[:, 512 : 512 + units] = ups.astype(bf16)
    mixed = rows.astype(f32) * inverse_gain_ref[...]
    squares = jnp.sum(mixed * mixed, axis=1, keepdims=True)
    high = squares.astype(bf16)
    squares = squares - high.astype(f32)
    middle = squares.astype(bf16)
    low = (squares - middle.astype(f32)).astype(bf16)
    for i, value in enumerate((high, middle, low)):
        out_ref[:, units + i : units + i + 1] = value


def gate_up(rows, inverse_gain, gates, ups):
    return pl.pallas_call(
        gate_up_body,
        in_specs=[pl.BlockSpec(memory_space=pltpu.VMEM)] * 4,
        out_specs=pl.BlockSpec(memory_space=pltpu.VMEM),
        out_shape=jax.ShapeDtypeStruct((rows.shape[0], 1024), bf16),
        compiler_params=pltpu.CompilerParams(vmem_limit_bytes=24 * 2**20),
    )(rows, inverse_gain, gates, ups)


def per_device(
    queries,
    prefix_cache,
    suffix_cache,
    suffix_lengths,
    residual,
    norm_gain,
    out_weight,
    gate_weight,
    up_weight,
    down_weight,
):
    rows, _, width = queries.shape
    units = gate_weight.shape[1]
    part = rows // X
    own, columns = residual.shape
    z_at = lax.axis_index("pb") % ZH * 8 + lax.axis_index("kv")
    own_rows = lax.dynamic_update_slice(
        jnp.zeros((2 * rows, columns), f32), residual, (z_at * own, 0)
    )
    block_gain = lax.dynamic_slice(norm_gain, (z_at % 8 * LANES,), (LANES,))
    prefix = lax.all_gather(prefix_cache[0], "rep", axis=1, tiled=True)
    group_queries = spread(queries[:, 0, :], 8, "pb")
    offset = lax.axis_index("pb") * suffix_cache.shape[3]
    highest, denoms, numers = local_attention(
        group_queries, prefix, suffix_cache[:, 0], suffix_lengths, offset
    )

    logs = highest + jnp.log(denoms)
    stats = jnp.pad(jnp.stack(split_float(logs), axis=1), ((0, 0), (0, 5), (0, width - rows)))
    parts = (numers / denoms[..., None]).astype(bf16)
    parts = exchange(jnp.concatenate([parts, stats], axis=1), "pb").astype(f32)
    logs = jnp.sum(parts[:, rows : rows + 3, :rows], axis=1)
    factor = jnp.exp(logs - jnp.max(logs, axis=0))
    factor = factor / jnp.sum(factor, axis=0)
    context = jnp.sum(parts[:, :rows] * factor[..., None], axis=0).astype(bf16)
    all_context = spread(context, 8, "rep").reshape(8, X, ZH, part // ZH, width)
    all_context = all_context.transpose(1, 2, 0, 3, 4).reshape(8 * rows, width)
    attended = jnp.dot(all_context, out_weight, preferred_element_type=f32).astype(bf16)
    attended = exchange(attended.reshape(X, 2 * rows, columns), "pb", x_groups)
    attended = jnp.sum(attended.astype(f32), axis=0)
    blocks = (attended + own_rows).astype(bf16).reshape(2, rows, Z // 2, LANES)
    blocks = blocks.swapaxes(1, 2).reshape(Z, rows, LANES)
    block = jnp.sum(exchange(blocks, ("kv", "pb"), z_groups).astype(f32), axis=0)
    block = (block * block_gain).astype(bf16)
    sent = spread(block, Z, ("kv", "pb"), z_groups).reshape(-1, LANES)
    sent = spread(sent, X, "pb", x_groups)
    scaled = sent.reshape(2 * X, Z // 2, rows, LANES).swapaxes(1, 2)
    scaled = scaled.reshape(8 * rows, columns)
    partial = gate_up(scaled, 1.0 / norm_gain[None], gate_weight.T, up_weight.T)
    partial = exchange(partial.reshape(8, rows, 1024), "rep")
    summed = jnp.sum(partial.astype(f32), axis=0)
    inverse = lax.rsqrt(jnp.sum(summed[:, units : units + 3], axis=1, keepdims=True) / D + epsilon)
    gates = summed[:, :units] * inverse
    ups = summed[:, 512 : 512 + units] * inverse
    hidden = (jax.nn.silu(gates) * ups).astype(bf16)
    hidden = spread(hidden, 8, "rep").reshape(8 * rows, units)
    out = jnp.dot(hidden, down_weight, preferred_element_type=f32).astype(bf16)
    out = exchange(out.reshape(X, 2 * rows, columns), "pb", x_groups)
    out = jnp.sum(out.astype(f32), axis=0) + attended
    out = exchange(out.astype(bf16).reshape(Z, -1, LANES), ("kv", "pb"), z_groups)
    out = jnp.sum(out.astype(f32), axis=0).reshape(own, columns)
    return (context[:, None, :], residual + out)


def solution(mesh):
    in_specs = (
        P("rep", ("kv", "pb"), None),
        P("kv", None, ("pb", "rep"), None),
        P("rep", "kv", None, "pb", None),
        P("rep"),
        P(("kv", "pb"), "rep"),
        P("rep"),
        P(("kv", "pb"), "rep"),
        P("rep", ("kv", "pb")),
        P("rep", ("kv", "pb")),
        P(("kv", "pb"), "rep"),
    )
    out_specs = (P("rep", ("kv", "pb"), None), P(("kv", "pb"), "rep"))
    return jax.shard_map(
        per_device, mesh=mesh, in_specs=in_specs, out_specs=out_specs, check_vma=False
    )
```

```python
import functools

import jax
import jax.numpy as jnp
from jax import lax
from jax.experimental import pallas as pl
from jax.experimental.pallas import tpu as pltpu
from jax.sharding import PartitionSpec as P

D = 8192
HEAD_DIM = 128
X = 4
ZH = 2
Z = 16
LANES = 128

lowest = -1e30
epsilon = 1e-06
f32 = jnp.float32
bf16 = jnp.bfloat16

x_groups = [[x * ZH + zh for x in range(X)] for zh in range(ZH)]
z_groups = [[kv * 8 + x * ZH + zh for zh in range(ZH) for kv in range(8)] for x in range(X)]


def exchange(blocks, axes, groups=None):
    return lax.all_to_all(blocks, axes, 0, 0, axis_index_groups=groups, tiled=True)


def spread(block, count, axes, groups=None):
    return exchange(jnp.broadcast_to(block[None], (count,) + block.shape), axes, groups)


def split_float(value):
    high = lax.reduce_precision(value, 8, 7)
    rest = value - high
    middle = lax.reduce_precision(rest, 8, 7)
    return high.astype(bf16), middle.astype(bf16), (rest - middle).astype(bf16)


def local_attention(queries, prefix, suffix, lengths, offset):
    scale = HEAD_DIM ** (-0.5)
    heads, rows, width = queries.shape
    shared = jnp.einsum("grd,td->grt", queries, prefix[0], preferred_element_type=f32) * scale
    own = jnp.einsum("grd,rsd->grs", queries, suffix[:, 0], preferred_element_type=f32) * scale
    position = offset + lax.broadcasted_iota(jnp.int32, (rows, suffix.shape[2]), 1)
    is_live = (position < lengths[:, None])[None]
    own = jnp.where(is_live, own, lowest)
    highest = jnp.maximum(jnp.max(shared, axis=2), jnp.max(own, axis=2))
    shared_weights = jnp.exp(shared - highest[..., None])
    own_weights = jnp.where(is_live, jnp.exp(own - highest[..., None]), 0.0)
    denoms = jnp.sum(shared_weights, axis=2) + jnp.sum(own_weights, axis=2)
    numers = jnp.einsum(
        "grt,td->grd", shared_weights.astype(bf16), prefix[1], preferred_element_type=f32
    ) + jnp.einsum(
        "grs,rsd->grd", own_weights.astype(bf16), suffix[:, 1], preferred_element_type=f32
    )
    return highest, denoms, numers


def merge_body(at_ref, parts_ref, residual_ref, blocks_ref, total_ref):
    total_ref[...] = sum(parts_ref[x].astype(f32) for x in range(X))
    rows = total_ref.shape[0]
    own = residual_ref.shape[0]
    place = lax.broadcasted_iota(jnp.int32, (rows, 1), 0) - at_ref[0]
    for j in range(Z // 2):
        columns = slice(j * LANES, (j + 1) * LANES)
        mixed = total_ref[:, columns]
        for i in range(own):
            mixed += jnp.where(place == i, residual_ref[i : i + 1, columns], 0.0)
        for half in range(2):
            blocks_ref[half * (Z // 2) + j] = mixed[
                half * (rows // 2) : (half + 1) * (rows // 2)
            ].astype(bf16)


def merge(at, parts, residual):
    _, rows, columns = parts.shape
    vmem = pl.BlockSpec(memory_space=pltpu.VMEM)
    return pl.pallas_call(
        merge_body,
        in_specs=[pl.BlockSpec(memory_space=pltpu.SMEM), vmem, vmem],
        out_specs=(vmem, vmem),
        out_shape=(
            jax.ShapeDtypeStruct((Z, rows // 2, LANES), bf16),
            jax.ShapeDtypeStruct((rows, columns), f32),
        ),
        compiler_params=pltpu.CompilerParams(vmem_limit_bytes=24 * 2**20),
    )(at, parts, residual)


def gate_up_body(blocks_ref, gain_ref, gate_ref, up_ref, out_ref, mixed_ref):
    units = gate_ref.shape[0]
    tiles = mixed_ref.shape[1] // LANES
    count = blocks_ref.shape[1]
    for i in range(blocks_ref.shape[0] // tiles):
        for j in range(tiles):
            mixed_ref[i * count : (i + 1) * count, j * LANES : (j + 1) * LANES] = blocks_ref[
                i * tiles + j
            ].astype(f32)
    mixed = mixed_ref[...]
    squares = jnp.sum(mixed * mixed, axis=1, keepdims=True)
    rows = (mixed * gain_ref[...]).astype(bf16)
    contract = (((1,), (1,)), ((), ()))
    gates = lax.dot_general(rows, gate_ref[...], contract, preferred_element_type=f32)
    out_ref[:, :units] = gates.astype(bf16)
    ups = lax.dot_general(rows, up_ref[...], contract, preferred_element_type=f32)
    out_ref[:, 512 : 512 + units] = ups.astype(bf16)
    high = squares.astype(bf16)
    squares = squares - high.astype(f32)
    middle = squares.astype(bf16)
    low = (squares - middle.astype(f32)).astype(bf16)
    for i, value in enumerate((high, middle, low)):
        out_ref[:, units + i : units + i + 1] = value


def gate_up(blocks, gain, gates, ups):
    columns = gain.shape[0]
    count = blocks.size // columns
    return pl.pallas_call(
        gate_up_body,
        in_specs=[pl.BlockSpec(memory_space=pltpu.VMEM)] * 4,
        out_specs=pl.BlockSpec(memory_space=pltpu.VMEM),
        out_shape=jax.ShapeDtypeStruct((count, 1024), bf16),
        scratch_shapes=[pltpu.VMEM((count, columns), f32)],
        compiler_params=pltpu.CompilerParams(vmem_limit_bytes=24 * 2**20),
    )(blocks, gain[None], gates, ups)


def per_device(
    queries,
    prefix_cache,
    suffix_cache,
    suffix_lengths,
    residual,
    norm_gain,
    out_weight,
    gate_weight,
    up_weight,
    down_weight,
):
    rows, _, width = queries.shape
    units = gate_weight.shape[1]
    part = rows // X
    own, columns = residual.shape
    z_at = lax.axis_index("pb") % ZH * 8 + lax.axis_index("kv")
    own_at = (z_at * own)[None]
    prefix = lax.all_gather(prefix_cache[0], "rep", axis=1, tiled=True)
    group_queries = spread(queries[:, 0, :], 8, "pb")
    offset = lax.axis_index("pb") * suffix_cache.shape[3]
    highest, denoms, numers = local_attention(
        group_queries, prefix, suffix_cache[:, 0], suffix_lengths, offset
    )

    logs = highest + jnp.log(denoms)
    stats = jnp.pad(jnp.stack(split_float(logs), axis=1), ((0, 0), (0, 5), (0, width - rows)))
    parts = (numers / denoms[..., None]).astype(bf16)
    parts, own_at = lax.optimization_barrier((jnp.concatenate([parts, stats], axis=1), own_at))
    parts = exchange(parts, "pb").astype(f32)
    logs = jnp.sum(parts[:, rows : rows + 3, :rows], axis=1)
    factor = jnp.exp(logs - jnp.max(logs, axis=0))
    factor = factor / jnp.sum(factor, axis=0)
    context = jnp.sum(parts[:, :rows] * factor[..., None], axis=0).astype(bf16)
    all_context = spread(context, 8, "rep").reshape(8, X, ZH, part // ZH, width)
    all_context = all_context.transpose(1, 2, 0, 3, 4).reshape(8 * rows, width)
    attended = jnp.dot(all_context, out_weight, preferred_element_type=f32).astype(bf16)
    attended = exchange(attended.reshape(X, 2 * rows, columns), "pb", x_groups)
    blocks, attended = merge(own_at, attended, residual)
    block = jnp.sum(exchange(blocks, ("kv", "pb"), z_groups).astype(f32), axis=0).astype(bf16)
    sent = spread(block, Z, ("kv", "pb"), z_groups).reshape(-1, LANES)
    sent = spread(sent, X, "pb", x_groups).reshape(-1, rows, LANES)
    partial = gate_up(sent, norm_gain, gate_weight.T, up_weight.T)
    partial = exchange(partial.reshape(8, rows, 1024), "rep")
    summed = jnp.sum(partial.astype(f32), axis=0)
    inverse = lax.rsqrt(jnp.sum(summed[:, units : units + 3], axis=1, keepdims=True) / D + epsilon)
    gates = summed[:, :units] * inverse
    ups = summed[:, 512 : 512 + units] * inverse
    hidden = (jax.nn.silu(gates) * ups).astype(bf16)
    hidden = spread(hidden, 8, "rep").reshape(8 * rows, units)
    out = jnp.dot(hidden, down_weight, preferred_element_type=f32).astype(bf16)
    out = exchange(out.reshape(X, 2 * rows, columns), "pb", x_groups)
    out = jnp.sum(out.astype(f32), axis=0) + attended
    out = exchange(out.astype(bf16).reshape(Z, -1, LANES), ("kv", "pb"), z_groups)
    out = jnp.sum(out.astype(f32), axis=0).reshape(own, columns)
    return (context[:, None, :], residual + out)


def solution(mesh):
    in_specs = (
        P("rep", ("kv", "pb"), None),
        P("kv", None, ("pb", "rep"), None),
        P("rep", "kv", None, "pb", None),
        P("rep"),
        P(("kv", "pb"), "rep"),
        P("rep"),
        P(("kv", "pb"), "rep"),
        P("rep", ("kv", "pb")),
        P("rep", ("kv", "pb")),
        P(("kv", "pb"), "rep"),
    )
    out_specs = (P("rep", ("kv", "pb"), None), P(("kv", "pb"), "rep"))
    return jax.shard_map(
        per_device, mesh=mesh, in_specs=in_specs, out_specs=out_specs, check_vma=False
    )
```

```python
import functools

import jax
import jax.numpy as jnp
from jax import lax
from jax.experimental import pallas as pl
from jax.experimental.pallas import tpu as pltpu
from jax.sharding import PartitionSpec as P

D = 8192
HEAD_DIM = 128
X = 4
ZH = 2
Z = 16
LANES = 128

lowest = -1e30
epsilon = 1e-06
f32 = jnp.float32
bf16 = jnp.bfloat16

x_groups = [[x * ZH + zh for x in range(X)] for zh in range(ZH)]
z_groups = [[kv * 8 + x * ZH + zh for zh in range(ZH) for kv in range(8)] for x in range(X)]


def exchange(blocks, axes, groups=None):
    return lax.all_to_all(blocks, axes, 0, 0, axis_index_groups=groups, tiled=True)


def spread(block, count, axes, groups=None):
    return exchange(jnp.broadcast_to(block[None], (count,) + block.shape), axes, groups)


def split_float(value):
    high = lax.reduce_precision(value, 8, 7)
    rest = value - high
    middle = lax.reduce_precision(rest, 8, 7)
    return high.astype(bf16), middle.astype(bf16), (rest - middle).astype(bf16)


def local_attention(queries, prefix, suffix, lengths, offset):
    scale = HEAD_DIM ** (-0.5)
    heads, rows, width = queries.shape
    count = suffix.shape[1] // 2
    shared = jnp.einsum("grd,td->grt", queries, prefix[0], preferred_element_type=f32) * scale
    own = jnp.einsum("grd,rsd->grs", queries, suffix, preferred_element_type=f32) * scale
    lane = lax.broadcasted_iota(jnp.int32, (rows, 2 * count), 1)
    is_live = ((lane < count) & (offset + lane < lengths[:, None]))[None]
    own = jnp.where(is_live, own, lowest)
    highest = jnp.maximum(jnp.max(shared, axis=2), jnp.max(own, axis=2))
    shared_weights = jnp.exp(shared - highest[..., None])
    own_weights = jnp.where(is_live, jnp.exp(own - highest[..., None]), 0.0)
    denoms = jnp.sum(shared_weights, axis=2) + jnp.sum(own_weights, axis=2)
    on_values = jnp.roll(own_weights.astype(bf16), count, axis=2)
    numers = jnp.einsum(
        "grt,td->grd", shared_weights.astype(bf16), prefix[1], preferred_element_type=f32
    ) + jnp.einsum("grs,rsd->grd", on_values, suffix, preferred_element_type=f32)
    return highest, denoms, numers


def merge_body(at_ref, parts_ref, residual_ref, blocks_ref, total_ref):
    total_ref[...] = sum(parts_ref[x].astype(f32) for x in range(X))
    rows = total_ref.shape[0]
    own = residual_ref.shape[0]
    place = lax.broadcasted_iota(jnp.int32, (rows, 1), 0) - at_ref[0]
    for j in range(Z // 2):
        columns = slice(j * LANES, (j + 1) * LANES)
        mixed = total_ref[:, columns]
        for i in range(own):
            mixed += jnp.where(place == i, residual_ref[i : i + 1, columns], 0.0)
        for half in range(2):
            blocks_ref[half * (Z // 2) + j] = mixed[
                half * (rows // 2) : (half + 1) * (rows // 2)
            ].astype(bf16)


def merge(at, parts, residual):
    _, rows, columns = parts.shape
    vmem = pl.BlockSpec(memory_space=pltpu.VMEM)
    return pl.pallas_call(
        merge_body,
        in_specs=[pl.BlockSpec(memory_space=pltpu.SMEM), vmem, vmem],
        out_specs=(vmem, vmem),
        out_shape=(
            jax.ShapeDtypeStruct((Z, rows // 2, LANES), bf16),
            jax.ShapeDtypeStruct((rows, columns), f32),
        ),
        compiler_params=pltpu.CompilerParams(vmem_limit_bytes=24 * 2**20),
    )(at, parts, residual)


def gate_up_body(blocks_ref, gain_ref, gate_ref, up_ref, out_ref, mixed_ref):
    units = gate_ref.shape[0]
    tiles = mixed_ref.shape[1] // LANES
    count = blocks_ref.shape[1]
    for i in range(blocks_ref.shape[0] // tiles):
        for j in range(tiles):
            mixed_ref[i * count : (i + 1) * count, j * LANES : (j + 1) * LANES] = blocks_ref[
                i * tiles + j
            ].astype(f32)
    mixed = mixed_ref[...]
    squares = jnp.sum(mixed * mixed, axis=1, keepdims=True)
    rows = (mixed * gain_ref[...]).astype(bf16)
    contract = (((1,), (1,)), ((), ()))
    gates = lax.dot_general(rows, gate_ref[...], contract, preferred_element_type=f32)
    out_ref[:, :units] = gates.astype(bf16)
    ups = lax.dot_general(rows, up_ref[...], contract, preferred_element_type=f32)
    out_ref[:, 512 : 512 + units] = ups.astype(bf16)
    high = squares.astype(bf16)
    squares = squares - high.astype(f32)
    middle = squares.astype(bf16)
    low = (squares - middle.astype(f32)).astype(bf16)
    for i, value in enumerate((high, middle, low)):
        out_ref[:, units + i : units + i + 1] = value


def gate_up(blocks, gain, gates, ups):
    columns = gain.shape[0]
    count = blocks.size // columns
    return pl.pallas_call(
        gate_up_body,
        in_specs=[pl.BlockSpec(memory_space=pltpu.VMEM)] * 4,
        out_specs=pl.BlockSpec(memory_space=pltpu.VMEM),
        out_shape=jax.ShapeDtypeStruct((count, 1024), bf16),
        scratch_shapes=[pltpu.VMEM((count, columns), f32)],
        compiler_params=pltpu.CompilerParams(vmem_limit_bytes=24 * 2**20),
    )(blocks, gain[None], gates, ups)


def per_device(
    queries,
    prefix_cache,
    suffix_cache,
    suffix_lengths,
    residual,
    norm_gain,
    out_weight,
    gate_weight,
    up_weight,
    down_weight,
):
    rows, _, width = queries.shape
    units = gate_weight.shape[1]
    part = rows // X
    own, columns = residual.shape
    z_at = lax.axis_index("pb") % ZH * 8 + lax.axis_index("kv")
    own_at = (z_at * own)[None]
    prefix = lax.all_gather(prefix_cache[0], "rep", axis=1, tiled=True)
    mine = queries[:, 0, :]
    other = lax.ppermute(mine, "pb", [(p, p ^ 1) for p in range(8)])
    other, prefix = lax.optimization_barrier((other, prefix))
    first = lax.axis_index("pb") % ZH == 0
    pair = jnp.stack([jnp.where(first, mine, other), jnp.where(first, other, mine)])
    group_queries = spread(pair, X, "pb", x_groups).reshape(8, rows, width)
    offset = lax.axis_index("pb") * suffix_cache.shape[3]
    highest, denoms, numers = local_attention(
        group_queries, prefix, suffix_cache.reshape(rows, -1, width), suffix_lengths, offset
    )

    logs = highest + jnp.log(denoms)
    stats = jnp.pad(jnp.stack(split_float(logs), axis=1), ((0, 0), (0, 5), (0, width - rows)))
    parts = (numers / denoms[..., None]).astype(bf16)
    parts, own_at = lax.optimization_barrier((jnp.concatenate([parts, stats], axis=1), own_at))
    parts = exchange(parts, "pb").astype(f32)
    logs = jnp.sum(parts[:, rows : rows + 3, :rows], axis=1)
    factor = jnp.exp(logs - jnp.max(logs, axis=0))
    factor = factor / jnp.sum(factor, axis=0)
    context = jnp.sum(parts[:, :rows] * factor[..., None], axis=0).astype(bf16)
    all_context = spread(context, 8, "rep").reshape(8, X, ZH, part // ZH, width)
    all_context = all_context.transpose(1, 2, 0, 3, 4).reshape(8 * rows, width)
    attended = jnp.dot(all_context, out_weight, preferred_element_type=f32).astype(bf16)
    attended = exchange(attended.reshape(X, 2 * rows, columns), "pb", x_groups)
    blocks, attended = merge(own_at, attended, residual)
    block = jnp.sum(exchange(blocks, ("kv", "pb"), z_groups).astype(f32), axis=0).astype(bf16)
    sent = spread(block, Z, ("kv", "pb"), z_groups).reshape(-1, LANES)
    sent = spread(sent, X, "pb", x_groups).reshape(-1, rows, LANES)
    partial = gate_up(sent, norm_gain, gate_weight.T, up_weight.T)
    partial = exchange(partial.reshape(8, rows, 1024), "rep")
    summed = jnp.sum(partial.astype(f32), axis=0)
    inverse = lax.rsqrt(jnp.sum(summed[:, units : units + 3], axis=1, keepdims=True) / D + epsilon)
    gates = summed[:, :units] * inverse
    ups = summed[:, 512 : 512 + units] * inverse
    hidden = (jax.nn.silu(gates) * ups).astype(bf16)
    hidden = spread(hidden, 8, "rep").reshape(8 * rows, units)
    out = jnp.dot(hidden, down_weight, preferred_element_type=f32).astype(bf16)
    out = exchange(out.reshape(X, 2 * rows, columns), "pb", x_groups)
    out = jnp.sum(out.astype(f32), axis=0) + attended
    out = exchange(out.astype(bf16).reshape(Z, -1, LANES), ("kv", "pb"), z_groups)
    out = jnp.sum(out.astype(f32), axis=0).reshape(own, columns)
    return (context[:, None, :], residual + out)


def solution(mesh):
    in_specs = (
        P("rep", ("kv", "pb"), None),
        P("kv", None, ("pb", "rep"), None),
        P("rep", "kv", None, "pb", None),
        P("rep"),
        P(("kv", "pb"), "rep"),
        P("rep"),
        P(("kv", "pb"), "rep"),
        P("rep", ("kv", "pb")),
        P("rep", ("kv", "pb")),
        P(("kv", "pb"), "rep"),
    )
    out_specs = (P("rep", ("kv", "pb"), None), P(("kv", "pb"), "rep"))
    return jax.shard_map(
        per_device, mesh=mesh, in_specs=in_specs, out_specs=out_specs, check_vma=False
    )
```

```python
import functools

import jax
import jax.numpy as jnp
from jax import lax
from jax.experimental import pallas as pl
from jax.experimental.pallas import tpu as pltpu
from jax.sharding import PartitionSpec as P

D = 8192
HEAD_DIM = 128
X = 4
ZH = 2
Z = 16
LANES = 128

lowest = -1e30
epsilon = 1e-06
f32 = jnp.float32
bf16 = jnp.bfloat16

x_groups = [[x * ZH + zh for x in range(X)] for zh in range(ZH)]
z_groups = [[kv * 8 + x * ZH + zh for zh in range(ZH) for kv in range(8)] for x in range(X)]


def exchange(blocks, axes, groups=None):
    return lax.all_to_all(blocks, axes, 0, 0, axis_index_groups=groups, tiled=True)


def spread(block, count, axes, groups=None):
    return exchange(jnp.broadcast_to(block[None], (count,) + block.shape), axes, groups)


def split_float(value):
    high = lax.reduce_precision(value, 8, 7)
    rest = value - high
    middle = lax.reduce_precision(rest, 8, 7)
    return high.astype(bf16), middle.astype(bf16), (rest - middle).astype(bf16)


def local_attention(queries, prefix, suffix, lane_bias):
    scale = HEAD_DIM ** (-0.5)
    heads, rows, width = queries.shape
    count = suffix.shape[1] // 2
    shared = jnp.einsum("grd,td->grt", queries, prefix[0], preferred_element_type=f32) * scale
    own = jnp.einsum("grd,rsd->grs", queries, suffix, preferred_element_type=f32) * scale
    own = own + lane_bias[None]
    highest = jnp.maximum(jnp.max(shared, axis=2), jnp.max(own, axis=2))
    shared_weights = jnp.exp(shared - highest[..., None])
    own_weights = jnp.exp(own - highest[..., None])
    denoms = jnp.sum(shared_weights, axis=2) + jnp.sum(own_weights, axis=2)
    on_values = jnp.roll(own_weights.astype(bf16), count, axis=2)
    numers = jnp.einsum(
        "grt,td->grd", shared_weights.astype(bf16), prefix[1], preferred_element_type=f32
    ) + jnp.einsum("grs,rsd->grd", on_values, suffix, preferred_element_type=f32)
    return highest, denoms, numers


def merge_body(at_ref, parts_ref, residual_ref, blocks_ref, total_ref):
    total_ref[...] = sum(parts_ref[x].astype(f32) for x in range(X))
    rows = total_ref.shape[0]
    own = residual_ref.shape[0]
    place = lax.broadcasted_iota(jnp.int32, (rows, 1), 0) - at_ref[0]
    for j in range(Z // 2):
        columns = slice(j * LANES, (j + 1) * LANES)
        mixed = total_ref[:, columns]
        for i in range(own):
            mixed += jnp.where(place == i, residual_ref[i : i + 1, columns], 0.0)
        for half in range(2):
            blocks_ref[half * (Z // 2) + j] = mixed[
                half * (rows // 2) : (half + 1) * (rows // 2)
            ].astype(bf16)


def merge(at, parts, residual):
    _, rows, columns = parts.shape
    vmem = pl.BlockSpec(memory_space=pltpu.VMEM)
    return pl.pallas_call(
        merge_body,
        in_specs=[pl.BlockSpec(memory_space=pltpu.SMEM), vmem, vmem],
        out_specs=(vmem, vmem),
        out_shape=(
            jax.ShapeDtypeStruct((Z, rows // 2, LANES), bf16),
            jax.ShapeDtypeStruct((rows, columns), f32),
        ),
        compiler_params=pltpu.CompilerParams(vmem_limit_bytes=24 * 2**20),
    )(at, parts, residual)


def gate_up_body(blocks_ref, gain_ref, gate_ref, up_ref, out_ref, mixed_ref):
    units = gate_ref.shape[0]
    tiles = mixed_ref.shape[1] // LANES
    count = blocks_ref.shape[1]
    for i in range(blocks_ref.shape[0] // tiles):
        for j in range(tiles):
            mixed_ref[i * count : (i + 1) * count, j * LANES : (j + 1) * LANES] = blocks_ref[
                i * tiles + j
            ].astype(f32)
    mixed = mixed_ref[...]
    squares = jnp.sum(mixed * mixed, axis=1, keepdims=True)
    rows = (mixed * gain_ref[...]).astype(bf16)
    contract = (((1,), (1,)), ((), ()))
    gates = lax.dot_general(rows, gate_ref[...], contract, preferred_element_type=f32)
    out_ref[:, :units] = gates.astype(bf16)
    ups = lax.dot_general(rows, up_ref[...], contract, preferred_element_type=f32)
    out_ref[:, 512 : 512 + units] = ups.astype(bf16)
    high = squares.astype(bf16)
    squares = squares - high.astype(f32)
    middle = squares.astype(bf16)
    low = (squares - middle.astype(f32)).astype(bf16)
    for i, value in enumerate((high, middle, low)):
        out_ref[:, units + i : units + i + 1] = value


def gate_up(blocks, gain, gates, ups):
    columns = gain.shape[0]
    count = blocks.size // columns
    return pl.pallas_call(
        gate_up_body,
        in_specs=[pl.BlockSpec(memory_space=pltpu.VMEM)] * 4,
        out_specs=pl.BlockSpec(memory_space=pltpu.VMEM),
        out_shape=jax.ShapeDtypeStruct((count, 1024), bf16),
        scratch_shapes=[pltpu.VMEM((count, columns), f32)],
        compiler_params=pltpu.CompilerParams(vmem_limit_bytes=24 * 2**20),
    )(blocks, gain[None], gates, ups)


def per_device(
    queries,
    prefix_cache,
    suffix_cache,
    suffix_lengths,
    residual,
    norm_gain,
    out_weight,
    gate_weight,
    up_weight,
    down_weight,
):
    rows, _, width = queries.shape
    units = gate_weight.shape[1]
    part = rows // X
    own, columns = residual.shape
    z_at = lax.axis_index("pb") % ZH * 8 + lax.axis_index("kv")
    own_at = (z_at * own)[None]
    prefix = lax.all_gather(prefix_cache[0], "rep", axis=1, tiled=True)
    mine = queries[:, 0, :]
    other = lax.ppermute(mine, "pb", [(p, p ^ 1) for p in range(8)])
    slots = suffix_cache.shape[3]
    lane = lax.broadcasted_iota(jnp.int32, (rows, 2 * slots), 1)
    position = lax.axis_index("pb") * slots + lane
    is_live = (lane < slots) & (position < suffix_lengths[:, None])
    lane_bias = jnp.where(is_live, 0.0, lowest).astype(f32)
    other, prefix, lane_bias, own_at = lax.optimization_barrier(
        (other, prefix, lane_bias, own_at)
    )
    first = lax.axis_index("pb") % ZH == 0
    pair = jnp.stack([jnp.where(first, mine, other), jnp.where(first, other, mine)])
    group_queries = spread(pair, X, "pb", x_groups).reshape(8, rows, width)
    highest, denoms, numers = local_attention(
        group_queries, prefix, suffix_cache.reshape(rows, -1, width), lane_bias
    )

    logs = highest + jnp.log(denoms)
    stats = jnp.pad(jnp.stack(split_float(logs), axis=1), ((0, 0), (0, 5), (0, width - rows)))
    parts = (numers / denoms[..., None]).astype(bf16)
    parts = jnp.concatenate([parts, stats], axis=1)
    parts = exchange(parts, "pb").astype(f32)
    logs = jnp.sum(parts[:, rows : rows + 3, :rows], axis=1)
    factor = jnp.exp(logs - jnp.max(logs, axis=0))
    factor = factor / jnp.sum(factor, axis=0)
    context = jnp.sum(parts[:, :rows] * factor[..., None], axis=0).astype(bf16)
    all_context = spread(context, 8, "rep").reshape(8, X, ZH, part // ZH, width)
    all_context = all_context.transpose(1, 2, 0, 3, 4).reshape(8 * rows, width)
    attended = jnp.dot(all_context, out_weight, preferred_element_type=f32).astype(bf16)
    attended = exchange(attended.reshape(X, 2 * rows, columns), "pb", x_groups)
    blocks, attended = merge(own_at, attended, residual)
    block = jnp.sum(exchange(blocks, ("kv", "pb"), z_groups).astype(f32), axis=0).astype(bf16)
    sent = spread(block, Z, ("kv", "pb"), z_groups).reshape(-1, LANES)
    sent = spread(sent, X, "pb", x_groups).reshape(-1, rows, LANES)
    partial = gate_up(sent, norm_gain, gate_weight.T, up_weight.T)
    partial = exchange(partial.reshape(8, rows, 1024), "rep")
    summed = jnp.sum(partial.astype(f32), axis=0)
    inverse = lax.rsqrt(jnp.sum(summed[:, units : units + 3], axis=1, keepdims=True) / D + epsilon)
    gates = summed[:, :units] * inverse
    ups = summed[:, 512 : 512 + units] * inverse
    hidden = (jax.nn.silu(gates) * ups).astype(bf16)
    hidden = spread(hidden, 8, "rep").reshape(8 * rows, units)
    out = jnp.dot(hidden, down_weight, preferred_element_type=f32).astype(bf16)
    out = exchange(out.reshape(X, 2 * rows, columns), "pb", x_groups)
    out = jnp.sum(out.astype(f32), axis=0) + attended
    out = exchange(out.astype(bf16).reshape(Z, -1, LANES), ("kv", "pb"), z_groups)
    out = jnp.sum(out.astype(f32), axis=0).reshape(own, columns)
    return (context[:, None, :], residual + out)


def solution(mesh):
    in_specs = (
        P("rep", ("kv", "pb"), None),
        P("kv", None, ("pb", "rep"), None),
        P("rep", "kv", None, "pb", None),
        P("rep"),
        P(("kv", "pb"), "rep"),
        P("rep"),
        P(("kv", "pb"), "rep"),
        P("rep", ("kv", "pb")),
        P("rep", ("kv", "pb")),
        P(("kv", "pb"), "rep"),
    )
    out_specs = (P("rep", ("kv", "pb"), None), P(("kv", "pb"), "rep"))
    return jax.shard_map(
        per_device, mesh=mesh, in_specs=in_specs, out_specs=out_specs, check_vma=False
    )
```
